32 devices in a mesh: seq: 8 (over z, core), rep: 4 (over y, x).
Axes of the slice: x: 2, y: 2, z: 4, core: 2. Of those that a mesh axis runs over, the one named last changes fastest.
Arguments:
- lengths: int32 [4], P('rep'), may hold values from 384 to 3072
- prompt_query: bfloat16 [4, 3072, 4096], P('rep', 'seq'), may hold values from -6 to 6
- prompt_key: bfloat16 [4, 3072, 4096], P('rep', 'seq'), may hold values from -0.52734375 to 0.52734375
- prompt_value: bfloat16 [4, 3072, 4096], P('rep', 'seq'), may hold values from -6 to 6
- prompt_decay: float32 [4, 32, 3072], P('rep', None, 'seq'), may hold values from -1 to 0
- step_query: bfloat16 [4, 4, 4096], P(None, 'rep', 'seq'), may hold values from -6 to 6
- step_key: bfloat16 [4, 4, 4096], P(None, 'rep', 'seq'), may hold values from -6 to 6
- step_value: bfloat16 [4, 4, 4096], P(None, 'rep', 'seq'), may hold values from -6 to 6
- step_decay: float32 [4, 4, 32], P(None, 'rep', 'seq'), may hold values from -1 to 0
- out_weight: bfloat16 [4096, 6144], P('seq', 'rep'), may hold values from -0.09375 to 0.09375
Outputs:
- prompt_out: bfloat16 [4, 3072, 4096], P('rep', 'seq')
- step_out: bfloat16 [4, 4, 6144], P(None, None, 'rep')
The draws below stay inside these ranges and needn't reach their ends.
All inputs are finite; a program needn't handle non-finite values.
Results may differ from the reference program's by a relative error of at most 0.0029.
The reference program's roundings to bfloat16 on the way count: a program that leaves them out, or rounds other values in their place, can miss the bound.
Values may be sent and summed in bfloat16 or wider, within the bound.
A program may use at most 128 MiB of HBM per device.

```python
import math
import jax
import jax.numpy as jnp
from jax import lax

HEADS = 32
HEAD_DIM = 128
D = 6144
TOK_DEV = 384
STEPS = 4
NUM_SEQUENCES = 4
PADDED_SPAN = 3072
N_SEQ = 8


def head_rates(key):
    base = jax.random.fold_in(key, 11)
    first, latter_portion, third = jax.random.split(base, 3)
    slow_share = 0.5
    slow_heads = jax.random.uniform(first, (HEADS,), jnp.float32) < slow_share
    slow_rate = jax.random.uniform(latter_portion, (HEADS,), jnp.float32, 0.2 / PADDED_SPAN, 2.0 / PADDED_SPAN)
    fast_rate = jnp.exp(jax.random.uniform(third, (HEADS,), jnp.float32, math.log(1.0 / 64.0), math.log(1.0 / 24.0)))
    return jnp.where(slow_heads, slow_rate, fast_rate)


def draw_prompt_decay(key, part):
    fading_speeds = head_rates(key)
    base = jax.random.fold_in(key, 23)
    first, latter_portion, third = jax.random.split(base, 3)
    jitter_shift = jax.random.uniform(first, (NUM_SEQUENCES, HEADS, PADDED_SPAN), jnp.float32, 0.5, 1.5)
    sequence_spans = (jax.random.uniform(latter_portion, (NUM_SEQUENCES, 1, PADDED_SPAN), jnp.float32) < 4.0 / PADDED_SPAN).astype(jnp.float32)
    fading_factor = jax.random.uniform(third, (NUM_SEQUENCES, HEADS, PADDED_SPAN), jnp.float32, 0.22, 0.69)
    return -fading_speeds[None, :, None] * jitter_shift - sequence_spans * fading_factor


def draw_step_decay(key, part):
    fading_speeds = head_rates(key)
    base = jax.random.fold_in(key, 37)
    jitter_shift = jax.random.uniform(base, (STEPS, NUM_SEQUENCES, HEADS), jnp.float32, 0.5, 1.5)
    return -fading_speeds[None, None, :] * jitter_shift


def plant(values, rng, smallest, high):
    longest = values.shape.index(max(values.shape))
    spots = []
    for shift in (0, 1):
        where = [jax.random.randint(jax.random.fold_in(rng, axis), (), 0, length) for axis, length in enumerate(values.shape)]
        where[longest] = (where[longest] + shift) % values.shape[longest]
        spots.append(tuple(where))
    return values.at[spots[0]].set(smallest).at[spots[1]].set(high)


def block_scale(rng, shape, cuts, smallest, top_value):
    level, own = 1.0, jax.random.fold_in(rng, 6)
    for axis_at, blocks in cuts:
        draws = jnp.exp(jax.random.uniform(jax.random.fold_in(own, axis_at), (blocks,), jnp.float32, smallest / len(cuts), top_value / len(cuts)))
        level = level * jnp.repeat(draws, shape[axis_at] // blocks).reshape([-1 if axis == axis_at else 1 for axis in range(len(shape))])
    return level


def scatter_about(own_key, dims, width, most, pieces=(), kind=jnp.bfloat16):
    result = width * jax.random.normal(own_key, dims, jnp.float32)
    if pieces:
        result = result * block_scale(own_key, dims, pieces, -0.22, 0.18)
    return jnp.clip(result, -most, most).astype(kind)


def setup_inputs(seed: int = 0) -> dict:
    keys = jax.random.split(jax.random.key(seed), 11)
    lengths = plant(jax.random.randint(keys[0], (NUM_SEQUENCES,), TOK_DEV, PADDED_SPAN + 1), jax.random.fold_in(keys[0], 1), TOK_DEV, PADDED_SPAN).astype(jnp.int32)
    prompt_query = scatter_about(keys[1], (NUM_SEQUENCES, PADDED_SPAN, HEADS * HEAD_DIM), 1.0, 6.0, ((0, 4), (1, 8)))
    prompt_key = scatter_about(keys[2], (NUM_SEQUENCES, PADDED_SPAN, HEADS * HEAD_DIM), 0.0884, 0.52734375, ((0, 4), (1, 8)))
    prompt_value = scatter_about(keys[3], (NUM_SEQUENCES, PADDED_SPAN, HEADS * HEAD_DIM), 1.0, 6.0, ((0, 4), (1, 8)))
    prompt_decay = draw_prompt_decay(jax.random.fold_in(keys[10], 71), 0)
    step_query = scatter_about(keys[5], (STEPS, NUM_SEQUENCES, HEADS * HEAD_DIM), 1.0, 6.0, ((1, 4), (2, 8)))
    step_key = scatter_about(keys[6], (STEPS, NUM_SEQUENCES, HEADS * HEAD_DIM), 1.0, 6.0, ((1, 4), (2, 8)))
    step_value = scatter_about(keys[7], (STEPS, NUM_SEQUENCES, HEADS * HEAD_DIM), 1.0, 6.0, ((1, 4), (2, 8)))
    step_decay = draw_step_decay(jax.random.fold_in(keys[10], 71), 0)
    out_weight = scatter_about(keys[9], (HEADS * HEAD_DIM, D), (HEADS * HEAD_DIM) ** -0.5, 0.09375, ((0, 8), (1, 4)))
    return dict(lengths=lengths, prompt_query=prompt_query, prompt_key=prompt_key, prompt_value=prompt_value, prompt_decay=prompt_decay, step_query=step_query, step_key=step_key, step_value=step_value, step_decay=step_decay, out_weight=out_weight)


epsilon = 1e-06

def block_attend(carry_in, block):
    query_rows, keys_in, value_input_rows, decay_in, live_mask = block
    log_decay = decay_in * live_mask[None, :]
    cumulative = jnp.cumsum(log_decay, axis=1)
    block_decay = cumulative[:, -1]
    keys_live = keys_in.astype(jnp.float32) * live_mask[:, None, None]
    scores = jnp.einsum('thd,shd->hts', query_rows.astype(jnp.float32), keys_live)
    offsets = jnp.arange(TOK_DEV, dtype=jnp.int32)
    causal = offsets[:, None] >= offsets[None, :]
    log_gaps = cumulative[:, :, None] - cumulative[:, None, :]
    decay_mask = jnp.where(causal[None], jnp.exp(jnp.where(causal[None], log_gaps, 0.0)), 0.0)
    weighted = (scores * decay_mask).astype(jnp.bfloat16)
    within = jnp.einsum('hts,shd->thd', weighted.astype(jnp.float32), value_input_rows.astype(jnp.float32))
    lower_carry_state = carry_in.astype(jnp.bfloat16)
    carried_state_term = jnp.einsum('cfx,fxi->cfi', query_rows.astype(jnp.float32), lower_carry_state.astype(jnp.float32))
    carried_state_term = carried_state_term * jnp.exp(cumulative).T[:, :, None]
    attended = (within + carried_state_term).reshape(TOK_DEV, HEADS * HEAD_DIM)
    normed = attended * lax.rsqrt(lax.optimization_barrier(jnp.mean(attended * attended, axis=-1, keepdims=True)) + epsilon) * live_mask[:, None]
    key_scaled_rows = (keys_live * jnp.exp(block_decay[None, :] - cumulative.T)[:, :, None]).astype(jnp.bfloat16)
    block_local_state = jnp.einsum('xjq,xjl->jql', key_scaled_rows.astype(jnp.float32), value_input_rows.astype(jnp.float32))
    carry_out = carry_in * jnp.exp(block_decay)[:, None, None] + block_local_state
    return (carry_out, normed.astype(jnp.bfloat16))

def one_prompt(items):
    length_one, query_one, key_one, value_one, decay_one = items
    live_all = (jnp.arange(PADDED_SPAN, dtype=jnp.int32) < length_one).astype(jnp.float32)
    shaped = (N_SEQ, TOK_DEV, HEADS, HEAD_DIM)
    blocks = (query_one.reshape(shaped), key_one.reshape(shaped), value_one.reshape(shaped), decay_one.reshape(HEADS, N_SEQ, TOK_DEV).transpose(1, 0, 2), live_all.reshape(N_SEQ, TOK_DEV))
    initial = jnp.zeros((HEADS, HEAD_DIM, HEAD_DIM), jnp.float32)
    final_state, outputs = lax.scan(block_attend, initial, blocks)
    return (final_state, outputs.reshape(PADDED_SPAN, HEADS * HEAD_DIM))

def reference(lengths, prompt_query, prompt_key, prompt_value, prompt_decay, step_query, step_key, step_value, step_decay, out_weight):
    final_states, prompt_out = lax.map(one_prompt, (lengths, prompt_query, prompt_key, prompt_value, prompt_decay))
    decode_state = final_states
    heard_list = []
    for step_num in range(STEPS):
        shaped = (NUM_SEQUENCES, HEADS, HEAD_DIM)
        step_q = step_query[step_num].reshape(shaped).astype(jnp.float32)
        step_k = step_key[step_num].reshape(shaped).astype(jnp.float32)
        step_v = step_value[step_num].reshape(shaped).astype(jnp.float32)
        decode_state = decode_state * jnp.exp(step_decay[step_num])[:, :, None, None] + step_k[:, :, :, None] * step_v[:, :, None, :]
        heard_now = jnp.einsum('rhk,rhkv->rhv', step_q, decode_state, precision=lax.Precision.HIGHEST)
        heard_list.append(heard_now.reshape(NUM_SEQUENCES, HEADS * HEAD_DIM))
    heard = jnp.stack(heard_list)
    normed = (heard * lax.rsqrt(lax.optimization_barrier(jnp.mean(heard * heard, axis=-1, keepdims=True)) + epsilon)).astype(jnp.bfloat16)
    projected = jnp.dot(normed.reshape(STEPS * NUM_SEQUENCES, HEADS * HEAD_DIM), out_weight, preferred_element_type=jnp.float32)
    step_out = projected.reshape(STEPS, NUM_SEQUENCES, D).astype(jnp.bfloat16)
    return (prompt_out, step_out)
```

```python
import functools
import jax
import jax.numpy as jnp
from jax import lax
from jax.experimental import pallas as pl
from jax.experimental.pallas import tpu as pltpu
from jax.sharding import PartitionSpec as P

HEAD_DIM = 128
CHUNK = 2
epsilon = 1e-06
MESH = pl.DeviceIdType.MESH
F32 = jnp.float32
BF16 = jnp.bfloat16


def dot(a, b, ca, cb, precision=None):
    return lax.dot_general(
        a, b, (((ca,), (cb,)), ((), ())), preferred_element_type=F32, precision=precision
    )


def prompt_kernel(
    n, heads, block,
    len_ref, q_ref, k_ref, v_ref, d_ref,
    out_ref, fin_ref,
    cum_b, cum_row, total, state, inbox, attended, squares, live_b,
    send_sem, recv_sem, fin_send, fin_recv,
):
    me = lax.axis_index("seq")
    rep = lax.axis_index("rep")
    last = n - 1
    share = heads // n
    chunk = min(CHUNK, share)
    chunks = heads // chunk
    per_owner = share // chunk

    barrier = pltpu.get_barrier_semaphore()
    for step in range(1, n):
        pl.semaphore_signal(
            barrier, inc=1, device_id=(lax.rem(me + step, n), rep), device_id_type=MESH
        )

    length = len_ref[0]
    start = me * block
    row_live = (lax.broadcasted_iota(jnp.int32, (1, block), 1) + start < length).astype(F32)
    live_b[...] = (
        lax.broadcasted_iota(jnp.int32, (block, HEAD_DIM), 0) + start < length
    ).astype(F32)
    log_decay = d_ref[0] * row_live
    below = (
        lax.broadcasted_iota(jnp.int32, (block, block), 0)
        >= lax.broadcasted_iota(jnp.int32, (block, block), 1)
    ).astype(F32)
    cum = dot(log_decay, below, 1, 1, lax.Precision.HIGHEST)
    for h in range(heads):
        cum_row[h] = cum[h : h + 1, :]
    cum_t = dot(below, log_decay, 1, 1, lax.Precision.HIGHEST)
    for h in range(heads):
        cum_b[h] = jnp.broadcast_to(cum_t[:, h : h + 1], (block, HEAD_DIM))
        total[h] = cum_b[h, block - 1 :, :]

    def columns(h):
        return pl.ds(pl.multiple_of(h * HEAD_DIM, HEAD_DIM), HEAD_DIM)

    def to_right(c):
        part = pl.ds(c * chunk, chunk)
        return pltpu.make_async_remote_copy(
            src_ref=state.at[part],
            dst_ref=inbox.at[part],
            send_sem=send_sem.at[c],
            recv_sem=recv_sem.at[c],
            device_id=(lax.rem(me + 1, n), rep),
            device_id_type=MESH,
        )

    def to_owner(c, owner):
        return pltpu.make_async_remote_copy(
            src_ref=state.at[pl.ds(c * chunk, chunk)],
            dst_ref=fin_ref.at[pl.ds((c % per_owner) * chunk, chunk)],
            send_sem=fin_send.at[c],
            recv_sem=fin_recv.at[c % per_owner],
            device_id=(owner, rep),
            device_id_type=MESH,
        )

    pl.semaphore_wait(barrier, n - 1)

    @pl.loop(0, chunks)
    def _(c):
        for i in range(chunk):
            h = c * chunk + i
            keys = k_ref[0, :, columns(h)].astype(F32) * live_b[...]
            scaled = (keys * jnp.exp(total[h] - cum_b[h])).astype(BF16)
            state[h] = dot(scaled, v_ref[0, :, columns(h)], 0, 0)

        @pl.when(me == 0)
        def _():
            to_right(c).start()

    tile = HEAD_DIM
    tiles = block // tile
    causal = (
        lax.broadcasted_iota(jnp.int32, (tile, tile), 0)
        >= lax.broadcasted_iota(jnp.int32, (tile, tile), 1)
    )
    squares[...] = jnp.zeros_like(squares)

    @pl.when(me == 0)
    def _():
        inbox[...] = jnp.zeros_like(inbox)

    @pl.loop(0, chunks)
    def _(c):
        @pl.when(me > 0)
        def _():
            to_right(c).wait_recv()
            for i in range(chunk):
                h = c * chunk + i
                state[h] = inbox[h] * jnp.exp(total[h]) + state[h]

            @pl.when(me < last)
            def _():
                to_right(c).start()

            @pl.when(me == last)
            def _():
                owner = c // per_owner

                @pl.when(owner != last)
                def _():
                    to_owner(c, owner).start()

                @pl.when(owner == last)
                def _():
                    fin_ref[pl.ds((c % per_owner) * chunk, chunk)] = state[
                        pl.ds(c * chunk, chunk)
                    ]

        for i in range(chunk):
            h = c * chunk + i
            query = q_ref[0, :, columns(h)]
            keys = (k_ref[0, :, columns(h)].astype(F32) * live_b[...]).astype(BF16)
            values = v_ref[0, :, columns(h)]
            carried = jnp.exp(cum_b[h]) * dot(query, inbox[h].astype(BF16), 1, 0)
            for t in range(tiles):
                rows = slice(t * tile, (t + 1) * tile)
                width = (t + 1) * tile
                scores = dot(query[rows], keys[:width], 1, 1)
                pieces = []
                for s in range(t + 1):
                    cols = slice(s * tile, (s + 1) * tile)
                    gap = cum_b[h, rows, :] - cum_row[h, :, cols]
                    if s == t:
                        decay = jnp.where(causal, jnp.exp(jnp.where(causal, gap, 0.0)), 0.0)
                    else:
                        decay = jnp.exp(gap)
                    pieces.append((scores[:, cols] * decay).astype(BF16))
                mixed = pieces[0] if t == 0 else jnp.concatenate(pieces, axis=1)
                both = dot(mixed, values[:width], 1, 0) + carried[rows]
                attended[rows, columns(h)] = both
                squares[rows, :] += both * both

    for t in range(tiles):
        rows = slice(t * tile, (t + 1) * tile)
        mean = jnp.sum(squares[rows, :], axis=1, keepdims=True) / (heads * HEAD_DIM)
        scale = jnp.broadcast_to(lax.rsqrt(mean + epsilon), (tile, HEAD_DIM)) * live_b[rows, :]
        squares[rows, :] = scale

    @pl.loop(0, heads)
    def _(h):
        out_ref[0, :, columns(h)] = (attended[:, columns(h)] * squares[...]).astype(BF16)

    @pl.when(me < last)
    def _():
        @pl.loop(0, chunks)
        def _(c):
            to_right(c).wait_send()

        @pl.loop(0, per_owner)
        def _(c):
            to_owner(c, last).wait_recv()

    @pl.when(me == last)
    def _():
        @pl.loop(0, chunks - per_owner)
        def _(c):
            to_owner(c, 0).wait_send()


def prompt_part(lengths, query, key, value, decay):
    n = lax.axis_size("seq")
    _, block, width = query.shape
    heads = width // HEAD_DIM
    share = heads // n
    chunk = min(CHUNK, share)
    vmem = pl.BlockSpec(memory_space=pltpu.VMEM)
    return pl.pallas_call(
        functools.partial(prompt_kernel, n, heads, block),
        out_shape=(
            jax.ShapeDtypeStruct(query.shape, BF16),
            jax.ShapeDtypeStruct((share, HEAD_DIM, HEAD_DIM), F32),
        ),
        in_specs=[pl.BlockSpec(memory_space=pltpu.SMEM)] + [vmem] * 4,
        out_specs=(vmem, vmem),
        scratch_shapes=[
            pltpu.VMEM((heads, block, HEAD_DIM), F32),
            pltpu.VMEM((heads, 1, block), F32),
            pltpu.VMEM((heads, 1, HEAD_DIM), F32),
            pltpu.VMEM((heads, HEAD_DIM, HEAD_DIM), F32),
            pltpu.VMEM((heads, HEAD_DIM, HEAD_DIM), F32),
            pltpu.VMEM((block, width), F32),
            pltpu.VMEM((block, HEAD_DIM), F32),
            pltpu.VMEM((block, HEAD_DIM), F32),
            pltpu.SemaphoreType.DMA((heads // chunk,)),
            pltpu.SemaphoreType.DMA((heads // chunk,)),
            pltpu.SemaphoreType.DMA((heads // chunk,)),
            pltpu.SemaphoreType.DMA((share // chunk,)),
        ],
        compiler_params=pltpu.CompilerParams(
            collective_id=0, has_side_effects=True, vmem_limit_bytes=52 * 1024 * 1024
        ),
    )(lengths, query, key, value, decay)


def shards(
    lengths,
    prompt_query,
    prompt_key,
    prompt_value,
    prompt_decay,
    step_query,
    step_key,
    step_value,
    step_decay,
    out_weight,
):
    feat_width = prompt_query.shape[2]
    prompt_out, final_state = prompt_part(
        lengths, prompt_query, prompt_key, prompt_value, prompt_decay
    )
    steps, reqs, part_width = step_query.shape
    share = part_width // HEAD_DIM
    shape = (steps, share, HEAD_DIM)
    q = step_query.reshape(shape).astype(F32)
    k = step_key.reshape(shape).astype(F32)
    v = step_value.reshape(shape).astype(F32)
    high = lax.Precision.HIGHEST
    at = jnp.arange(steps)
    causal = (at[:, None] >= at[None, :])[:, :, None]
    cum = jnp.sum(jnp.where(causal, step_decay.reshape(steps, share)[None], 0.0), axis=1)
    gaps = jnp.where(causal, cum[:, None, :] - cum[None, :, :], 0.0)
    weights = jnp.where(causal, jnp.exp(gaps), 0.0)
    own = jnp.sum(q[:, None] * k[None, :], axis=-1) * weights
    fresh = jnp.sum(own[:, :, :, None] * v[None, :], axis=1)
    kept = jnp.einsum("shk,hkv->shv", q, final_state, precision=high)
    heard = (kept * jnp.exp(cum)[:, :, None] + fresh).reshape(steps, reqs, part_width)
    sum_squares = lax.psum(jnp.sum(heard * heard, axis=-1), "seq")
    normed = (heard * lax.rsqrt(sum_squares[:, :, None] / feat_width + epsilon)).astype(BF16)
    projected = jnp.einsum(
        "srf,fc->src",
        lax.all_gather(normed, "rep", axis=1, tiled=True),
        out_weight,
        preferred_element_type=F32,
    )
    step_out = lax.psum(projected, "seq").astype(BF16)
    return (prompt_out, step_out)


def solution(mesh):
    return jax.shard_map(
        shards,
        mesh=mesh,
        in_specs=(
            P("rep"),
            P("rep", "seq", None),
            P("rep", "seq", None),
            P("rep", "seq", None),
            P("rep", None, "seq"),
            P(None, "rep", "seq"),
            P(None, "rep", "seq"),
            P(None, "rep", "seq"),
            P(None, "rep", "seq"),
            P("seq", "rep"),
        ),
        out_specs=(P("rep", "seq", None), P(None, None, "rep")),
        check_vma=False,
    )
```

```python
import functools
import jax
import jax.numpy as jnp
from jax import lax
from jax.experimental import pallas as pl
from jax.experimental.pallas import tpu as pltpu
from jax.sharding import PartitionSpec as P

HEAD_DIM = 128
CHUNK = 2
epsilon = 1e-06
MESH = pl.DeviceIdType.MESH
F32 = jnp.float32
BF16 = jnp.bfloat16


def dot(a, b, ca, cb, precision=None):
    return lax.dot_general(
        a, b, (((ca,), (cb,)), ((), ())), preferred_element_type=F32, precision=precision
    )


def prompt_kernel(
    n, reps, heads, block,
    len_ref, q_ref, k_ref, v_ref, d_ref, sq_ref, sk_ref, sv_ref, sd_ref, w_ref,
    out_ref, step_ref,
    fin_ref, heard, ssq_all, norm_all, rows_in, parts, parts_in, sums, rows_out,
    cum_b, cum_row, total, state, inbox, attended, squares, live_b,
    send_sem, recv_sem, fin_send, fin_recv,
    ssq_send, ssq_recv, norm_send, norm_recv, part_send, part_recv, sum_send, sum_recv,
):
    me = lax.axis_index("seq")
    rep = lax.axis_index("rep")
    last = n - 1
    share = heads // n
    chunk = min(CHUNK, share)
    chunks = heads // chunk
    per_owner = share // chunk

    barrier = pltpu.get_barrier_semaphore()
    for step in range(1, n):
        pl.semaphore_signal(
            barrier, inc=1, device_id=(lax.rem(me + step, n), rep), device_id_type=MESH
        )

    for step in range(1, reps):
        pl.semaphore_signal(
            barrier, inc=1, device_id=(me, lax.rem(rep + step, reps)), device_id_type=MESH
        )

    length = len_ref[0]
    start = me * block
    row_live = (lax.broadcasted_iota(jnp.int32, (1, block), 1) + start < length).astype(F32)
    live_b[...] = (
        lax.broadcasted_iota(jnp.int32, (block, HEAD_DIM), 0) + start < length
    ).astype(F32)
    log_decay = d_ref[0] * row_live
    below = (
        lax.broadcasted_iota(jnp.int32, (block, block), 0)
        >= lax.broadcasted_iota(jnp.int32, (block, block), 1)
    ).astype(F32)
    cum = dot(log_decay, below, 1, 1, lax.Precision.HIGHEST)
    for h in range(heads):
        cum_row[h] = cum[h : h + 1, :]
    cum_t = dot(below, log_decay, 1, 1, lax.Precision.HIGHEST)
    for h in range(heads):
        cum_b[h] = jnp.broadcast_to(cum_t[:, h : h + 1], (block, HEAD_DIM))
        total[h] = cum_b[h, block - 1 :, :]

    def columns(h):
        return pl.ds(pl.multiple_of(h * HEAD_DIM, HEAD_DIM), HEAD_DIM)

    def to_right(c):
        part = pl.ds(c * chunk, chunk)
        return pltpu.make_async_remote_copy(
            src_ref=state.at[part],
            dst_ref=inbox.at[part],
            send_sem=send_sem.at[c],
            recv_sem=recv_sem.at[c],
            device_id=(lax.rem(me + 1, n), rep),
            device_id_type=MESH,
        )

    def to_owner(c, owner):
        return pltpu.make_async_remote_copy(
            src_ref=state.at[pl.ds(c * chunk, chunk)],
            dst_ref=fin_ref.at[pl.ds((c % per_owner) * chunk, chunk)],
            send_sem=fin_send.at[c],
            recv_sem=fin_recv.at[c % per_owner],
            device_id=(owner, rep),
            device_id_type=MESH,
        )

    pl.semaphore_wait(barrier, n - 1 + reps - 1)

    @pl.loop(0, chunks)
    def _(c):
        for i in range(chunk):
            h = c * chunk + i
            keys = k_ref[0, :, columns(h)].astype(F32) * live_b[...]
            scaled = (keys * jnp.exp(total[h] - cum_b[h])).astype(BF16)
            state[h] = dot(scaled, v_ref[0, :, columns(h)], 0, 0)

        @pl.when(me == 0)
        def _():
            to_right(c).start()

    tile = HEAD_DIM
    tiles = block // tile
    causal = (
        lax.broadcasted_iota(jnp.int32, (tile, tile), 0)
        >= lax.broadcasted_iota(jnp.int32, (tile, tile), 1)
    )
    squares[...] = jnp.zeros_like(squares)

    @pl.when(me == 0)
    def _():
        inbox[...] = jnp.zeros_like(inbox)

    @pl.loop(0, chunks)
    def _(c):
        @pl.when(me > 0)
        def _():
            to_right(c).wait_recv()
            for i in range(chunk):
                h = c * chunk + i
                state[h] = inbox[h] * jnp.exp(total[h]) + state[h]

            @pl.when(me < last)
            def _():
                to_right(c).start()

            @pl.when(me == last)
            def _():
                owner = c // per_owner

                @pl.when(owner != last)
                def _():
                    to_owner(c, owner).start()

                @pl.when(owner == last)
                def _():
                    fin_ref[pl.ds((c % per_owner) * chunk, chunk)] = state[
                        pl.ds(c * chunk, chunk)
                    ]

        for i in range(chunk):
            h = c * chunk + i
            query = q_ref[0, :, columns(h)]
            keys = (k_ref[0, :, columns(h)].astype(F32) * live_b[...]).astype(BF16)
            values = v_ref[0, :, columns(h)]
            carried = jnp.exp(cum_b[h]) * dot(query, inbox[h].astype(BF16), 1, 0)
            for t in range(tiles):
                rows = slice(t * tile, (t + 1) * tile)
                width = (t + 1) * tile
                scores = dot(query[rows], keys[:width], 1, 1)
                pieces = []
                for s in range(t + 1):
                    cols = slice(s * tile, (s + 1) * tile)
                    gap = cum_b[h, rows, :] - cum_row[h, :, cols]
                    if s == t:
                        decay = jnp.where(causal, jnp.exp(jnp.where(causal, gap, 0.0)), 0.0)
                    else:
                        decay = jnp.exp(gap)
                    pieces.append((scores[:, cols] * decay).astype(BF16))
                mixed = pieces[0] if t == 0 else jnp.concatenate(pieces, axis=1)
                both = dot(mixed, values[:width], 1, 0) + carried[rows]
                attended[rows, columns(h)] = both
                squares[rows, :] += both * both

    for t in range(tiles):
        rows = slice(t * tile, (t + 1) * tile)
        mean = jnp.sum(squares[rows, :], axis=1, keepdims=True) / (heads * HEAD_DIM)
        scale = jnp.broadcast_to(lax.rsqrt(mean + epsilon), (tile, HEAD_DIM)) * live_b[rows, :]
        squares[rows, :] = scale

    def scale_out(first, end):
        @pl.loop(first, end)
        def _(h):
            out_ref[0, :, columns(h)] = (attended[:, columns(h)] * squares[...]).astype(BF16)

    def along_seq(source, target, sends, receives, step, slot, arriving):
        peer = lax.rem(me + step, n)
        landing = peer if arriving else me
        return pltpu.make_async_remote_copy(
            src_ref=source.at[peer if slot else me],
            dst_ref=target.at[landing],
            send_sem=sends.at[step],
            recv_sem=receives.at[landing],
            device_id=(peer, rep),
            device_id_type=MESH,
        )

    def along_rep(step, arriving):
        peer = lax.rem(rep + step, reps)
        landing = peer if arriving else rep
        return pltpu.make_async_remote_copy(
            src_ref=norm_all.at[rep],
            dst_ref=norm_all.at[landing],
            send_sem=norm_send.at[step],
            recv_sem=norm_recv.at[landing],
            device_id=(me, peer),
            device_id_type=MESH,
        )

    @pl.when(me < last)
    def _():
        @pl.loop(0, per_owner)
        def _(c):
            to_owner(c, last).wait_recv()

    steps = sq_ref.shape[0]
    heard[...] = jnp.zeros_like(heard)
    for i in range(share):
        cols = slice(i * HEAD_DIM, (i + 1) * HEAD_DIM)
        queries = [sq_ref[s, :, cols].astype(F32) for s in range(steps)]
        keys = [sk_ref[s, :, cols].astype(F32) for s in range(steps)]
        values = [sv_ref[s, :, cols].astype(F32) for s in range(steps)]
        cums = []
        for s in range(steps):
            one = sd_ref[s, :, i : i + 1]
            cums.append(one if s == 0 else cums[-1] + one)
        for s in range(steps):
            heard[s : s + 1, cols] = queries[s]
        kept = dot(heard[:, cols], fin_ref[i], 1, 0, lax.Precision.HIGHEST)
        for s in range(steps):
            row = jnp.exp(cums[s]) * kept[s : s + 1, :]
            for j in range(s + 1):
                meet = jnp.sum(queries[s] * keys[j], axis=1, keepdims=True)
                row = row + (meet * jnp.exp(cums[s] - cums[j])) * values[j]
            heard[s : s + 1, cols] = row
    mine = heard[:steps, :]
    ssq_all[me] = jnp.broadcast_to(jnp.sum(mine * mine, axis=1, keepdims=True), (steps, HEAD_DIM))
    for step in range(1, n):
        along_seq(ssq_all, ssq_all, ssq_send, ssq_recv, step, False, False).start()
    cut = heads // 3
    scale_out(0, cut)
    for step in range(1, n):
        along_seq(ssq_all, ssq_all, ssq_send, ssq_recv, step, False, True).wait_recv()
    mean = jnp.sum(ssq_all[...], axis=0)[:, :1] / (heads * HEAD_DIM)
    norm_all[rep] = (mine * lax.rsqrt(mean + epsilon)).astype(BF16).astype(F32)
    for step in range(1, reps):
        along_rep(step, False).start()
    scale_out(cut, 2 * cut)
    for step in range(1, reps):
        along_rep(step, True).wait_recv()
    for r in range(reps):
        for s in range(steps):
            at = s * reps + r
            rows_in[at : at + 1, :] = norm_all[r, s : s + 1, :]
    projected = dot(rows_in[...].astype(BF16), w_ref[...], 1, 0)
    per = steps * reps // n
    for j in range(n):
        parts[j] = projected[j * per : (j + 1) * per, :]
    for step in range(1, n):
        along_seq(parts, parts_in, part_send, part_recv, step, True, False).start()
    parts_in[me] = parts[me]
    scale_out(2 * cut, heads)
    for step in range(1, n):
        along_seq(parts, parts_in, part_send, part_recv, step, True, True).wait_recv()
    sums[me] = jnp.sum(parts_in[...], axis=0)
    for step in range(1, n):
        along_seq(sums, sums, sum_send, sum_recv, step, False, False).start()
    for step in range(1, n):
        along_seq(sums, sums, sum_send, sum_recv, step, False, True).wait_recv()
    for j in range(n):
        rows_out[j * per : (j + 1) * per, :] = sums[j]
    step_ref[...] = rows_out[...].astype(BF16)

    for step in range(1, n):
        along_seq(ssq_all, ssq_all, ssq_send, ssq_recv, step, False, False).wait_send()
        along_seq(parts, parts_in, part_send, part_recv, step, True, False).wait_send()
        along_seq(sums, sums, sum_send, sum_recv, step, False, False).wait_send()
    for step in range(1, reps):
        along_rep(step, False).wait_send()

    @pl.when(me < last)
    def _():
        @pl.loop(0, chunks)
        def _(c):
            to_right(c).wait_send()

    @pl.when(me == last)
    def _():
        @pl.loop(0, chunks - per_owner)
        def _(c):
            to_owner(c, 0).wait_send()


def whole(lengths, query, key, value, decay, *decoding):
    n, reps = lax.axis_size("seq"), lax.axis_size("rep")
    _, block, width = query.shape
    heads = width // HEAD_DIM
    share = heads // n
    chunk = min(CHUNK, share)
    steps, _, part_width = decoding[0].shape
    out_columns = decoding[-1].shape[1]
    rows = steps * reps
    vmem = pl.BlockSpec(memory_space=pltpu.VMEM)
    return pl.pallas_call(
        functools.partial(prompt_kernel, n, reps, heads, block),
        out_shape=(
            jax.ShapeDtypeStruct(query.shape, BF16),
            jax.ShapeDtypeStruct((rows, out_columns), BF16),
        ),
        in_specs=[pl.BlockSpec(memory_space=pltpu.SMEM)] + [vmem] * 9,
        out_specs=(vmem, vmem),
        scratch_shapes=[
            pltpu.VMEM((share, HEAD_DIM, HEAD_DIM), F32),
            pltpu.VMEM((8 * pl.cdiv(steps, 8), part_width), F32),
            pltpu.VMEM((n, steps, HEAD_DIM), F32),
            pltpu.VMEM((reps, steps, part_width), F32),
            pltpu.VMEM((rows, part_width), F32),
            pltpu.VMEM((n, rows // n, out_columns), F32),
            pltpu.VMEM((n, rows // n, out_columns), F32),
            pltpu.VMEM((n, rows // n, out_columns), F32),
            pltpu.VMEM((rows, out_columns), F32),
            pltpu.VMEM((heads, block, HEAD_DIM), F32),
            pltpu.VMEM((heads, 1, block), F32),
            pltpu.VMEM((heads, 1, HEAD_DIM), F32),
            pltpu.VMEM((heads, HEAD_DIM, HEAD_DIM), F32),
            pltpu.VMEM((heads, HEAD_DIM, HEAD_DIM), F32),
            pltpu.VMEM((block, width), F32),
            pltpu.VMEM((block, HEAD_DIM), F32),
            pltpu.VMEM((block, HEAD_DIM), F32),
            pltpu.SemaphoreType.DMA((heads // chunk,)),
            pltpu.SemaphoreType.DMA((heads // chunk,)),
            pltpu.SemaphoreType.DMA((heads // chunk,)),
            pltpu.SemaphoreType.DMA((share // chunk,)),
            pltpu.SemaphoreType.DMA((n,)),
            pltpu.SemaphoreType.DMA((n,)),
            pltpu.SemaphoreType.DMA((reps,)),
            pltpu.SemaphoreType.DMA((reps,)),
            pltpu.SemaphoreType.DMA((n,)),
            pltpu.SemaphoreType.DMA((n,)),
            pltpu.SemaphoreType.DMA((n,)),
            pltpu.SemaphoreType.DMA((n,)),
        ],
        compiler_params=pltpu.CompilerParams(
            collective_id=0, has_side_effects=True, vmem_limit_bytes=52 * 1024 * 1024
        ),
    )(lengths, query, key, value, decay, *decoding)


def shards(
    lengths,
    prompt_query,
    prompt_key,
    prompt_value,
    prompt_decay,
    step_query,
    step_key,
    step_value,
    step_decay,
    out_weight,
):
    prompt_out, rows = whole(
        lengths,
        prompt_query,
        prompt_key,
        prompt_value,
        prompt_decay,
        step_query,
        step_key,
        step_value,
        step_decay,
        out_weight,
    )
    steps = step_query.shape[0]
    return (prompt_out, rows.reshape(steps, rows.shape[0] // steps, rows.shape[1]))


def solution(mesh):
    return jax.shard_map(
        shards,
        mesh=mesh,
        in_specs=(
            P("rep"),
            P("rep", "seq", None),
            P("rep", "seq", None),
            P("rep", "seq", None),
            P("rep", None, "seq"),
            P(None, "rep", "seq"),
            P(None, "rep", "seq"),
            P(None, "rep", "seq"),
            P(None, "rep", "seq"),
            P("seq", "rep"),
        ),
        out_specs=(P("rep", "seq", None), P(None, None, "rep")),
        check_vma=False,
    )
```

```python
import functools
import jax
import jax.numpy as jnp
from jax import lax
from jax.experimental import pallas as pl
from jax.experimental.pallas import tpu as pltpu
from jax.sharding import PartitionSpec as P

HEAD_DIM = 128
CHUNK = 1
epsilon = 1e-06
MESH = pl.DeviceIdType.MESH
F32 = jnp.float32
BF16 = jnp.bfloat16


def dot(a, b, ca, cb, precision=None):
    return lax.dot_general(
        a, b, (((ca,), (cb,)), ((), ())), preferred_element_type=F32, precision=precision
    )


def prompt_kernel(
    n, reps, heads, block,
    len_ref, q_hbm, k_hbm, v_hbm, d_hbm, step_in, sd_ref, w_hbm,
    out_ref, step_ref,
    q_ref, k_ref, v_ref, d_ref, w_ref, load_sem, gains, fresh,
    fin_ref, heard, ssq_all, norm_all, rows_in, parts, parts_in, sums, rows_out,
    cum_b, cum_row, total, state, inbox, attended, squares, live_b,
    send_sem, recv_sem, fin_send, fin_recv,
    ssq_send, ssq_recv, norm_send, norm_recv, part_send, part_recv, sum_send, sum_recv,
):
    me = lax.axis_index("seq")
    rep = lax.axis_index("rep")
    last = n - 1
    share = heads // n
    chunk = min(CHUNK, share)
    chunks = heads // chunk
    per_owner = share // chunk

    loads = [
        pltpu.make_async_copy(source, target, load_sem.at[i])
        for i, (source, target) in enumerate(
            (
                (d_hbm, d_ref),
                (k_hbm, k_ref),
                (v_hbm, v_ref),
                (q_hbm, q_ref),
                (w_hbm, w_ref),
            )
        )
    ]
    for load in loads:
        load.start()
    barrier = pltpu.get_barrier_semaphore()
    for step in range(1, n):
        pl.semaphore_signal(
            barrier, inc=1, device_id=(lax.rem(me + step, n), rep), device_id_type=MESH
        )

    for step in range(1, reps):
        pl.semaphore_signal(
            barrier, inc=1, device_id=(me, lax.rem(rep + step, reps)), device_id_type=MESH
        )

    length = len_ref[0]
    start = me * block
    row_live = (lax.broadcasted_iota(jnp.int32, (1, block), 1) + start < length).astype(F32)
    live_b[...] = (
        lax.broadcasted_iota(jnp.int32, (block, HEAD_DIM), 0) + start < length
    ).astype(F32)
    loads[0].wait()
    log_decay = d_ref[0] * row_live
    below = (
        lax.broadcasted_iota(jnp.int32, (block, block), 0)
        >= lax.broadcasted_iota(jnp.int32, (block, block), 1)
    ).astype(F32)
    cum = dot(log_decay, below, 1, 1, lax.Precision.HIGHEST)
    for h in range(heads):
        cum_row[h] = cum[h : h + 1, :]
    cum_t = dot(below, log_decay, 1, 1, lax.Precision.HIGHEST)
    for h in range(heads):
        cum_b[h] = jnp.broadcast_to(cum_t[:, h : h + 1], (block, HEAD_DIM))
        total[h] = cum_b[h, block - 1 :, :]

    def columns(h):
        return pl.ds(pl.multiple_of(h * HEAD_DIM, HEAD_DIM), HEAD_DIM)

    def to_right(c):
        part = pl.ds(c * chunk, chunk)
        return pltpu.make_async_remote_copy(
            src_ref=state.at[part],
            dst_ref=inbox.at[part],
            send_sem=send_sem.at[c],
            recv_sem=recv_sem.at[c],
            device_id=(lax.rem(me + 1, n), rep),
            device_id_type=MESH,
        )

    def to_owner(c, owner):
        return pltpu.make_async_remote_copy(
            src_ref=state.at[pl.ds(c * chunk, chunk)],
            dst_ref=fin_ref.at[pl.ds((c % per_owner) * chunk, chunk)],
            send_sem=fin_send.at[c],
            recv_sem=fin_recv.at[c % per_owner],
            device_id=(owner, rep),
            device_id_type=MESH,
        )

    loads[1].wait()
    loads[2].wait()
    pl.semaphore_wait(barrier, n - 1 + reps - 1)

    @pl.loop(0, chunks)
    def _(c):
        for i in range(chunk):
            h = c * chunk + i
            keys = k_ref[0, :, columns(h)].astype(F32) * live_b[...]
            scaled = (keys * jnp.exp(total[h] - cum_b[h])).astype(BF16)
            state[h] = dot(scaled, v_ref[0, :, columns(h)], 0, 0)

        @pl.when(me == 0)
        def _():
            to_right(c).start()

    loads[3].wait()
    loads[4].wait()
    steps = step_in.shape[0] // 3
    heard[...] = jnp.zeros_like(heard)
    gains[...] = jnp.zeros_like(gains)
    fresh[...] = jnp.zeros_like(fresh)
    heard[:steps, :] = step_in[:steps, :]
    for i in range(share):
        cols = slice(i * HEAD_DIM, (i + 1) * HEAD_DIM)
        cums = []
        for s in range(steps):
            one = sd_ref[s, :, i : i + 1]
            cums.append(one if s == 0 else cums[-1] + one)
            row = jnp.zeros((1, HEAD_DIM), F32)
            for j in range(s + 1):
                met = step_in[s : s + 1, cols] * step_in[steps + j : steps + j + 1, cols]
                meet = jnp.sum(met, axis=1, keepdims=True) * jnp.exp(cums[s] - cums[j])
                row = row + meet * step_in[2 * steps + j : 2 * steps + j + 1, cols]
            fresh[s : s + 1, cols] = row
            gains[s : s + 1, cols] = jnp.broadcast_to(jnp.exp(cums[s]), (1, HEAD_DIM))

    tile = HEAD_DIM
    tiles = block // tile
    causal = (
        lax.broadcasted_iota(jnp.int32, (tile, tile), 0)
        >= lax.broadcasted_iota(jnp.int32, (tile, tile), 1)
    )
    squares[...] = jnp.zeros_like(squares)

    @pl.when(me == 0)
    def _():
        inbox[...] = jnp.zeros_like(inbox)

    @pl.loop(0, chunks)
    def _(c):
        @pl.when(me > 0)
        def _():
            to_right(c).wait_recv()
            for i in range(chunk):
                h = c * chunk + i
                state[h] = inbox[h] * jnp.exp(total[h]) + state[h]

            @pl.when(me < last)
            def _():
                to_right(c).start()

            @pl.when(me == last)
            def _():
                owner = c // per_owner

                @pl.when(owner != last)
                def _():
                    to_owner(c, owner).start()

                @pl.when(owner == last)
                def _():
                    fin_ref[pl.ds((c % per_owner) * chunk, chunk)] = state[
                        pl.ds(c * chunk, chunk)
                    ]

        for i in range(chunk):
            h = c * chunk + i
            query = q_ref[0, :, columns(h)]
            keys = (k_ref[0, :, columns(h)].astype(F32) * live_b[...]).astype(BF16)
            values = v_ref[0, :, columns(h)]
            carried = jnp.exp(cum_b[h]) * dot(query, inbox[h].astype(BF16), 1, 0)
            for t in range(tiles):
                rows = slice(t * tile, (t + 1) * tile)
                width = (t + 1) * tile
                scores = dot(query[rows], keys[:width], 1, 1)
                pieces = []
                for s in range(t + 1):
                    cols = slice(s * tile, (s + 1) * tile)
                    gap = cum_b[h, rows, :] - cum_row[h, :, cols]
                    if s == t:
                        decay = jnp.where(causal, jnp.exp(jnp.where(causal, gap, 0.0)), 0.0)
                    else:
                        decay = jnp.exp(gap)
                    pieces.append((scores[:, cols] * decay).astype(BF16))
                mixed = pieces[0] if t == 0 else jnp.concatenate(pieces, axis=1)
                both = dot(mixed, values[:width], 1, 0) + carried[rows]
                attended[rows, columns(h)] = both
                squares[rows, :] += both * both

    for t in range(tiles):
        rows = slice(t * tile, (t + 1) * tile)
        mean = jnp.sum(squares[rows, :], axis=1, keepdims=True) / (heads * HEAD_DIM)
        scale = jnp.broadcast_to(lax.rsqrt(mean + epsilon), (tile, HEAD_DIM)) * live_b[rows, :]
        squares[rows, :] = scale

    def scale_out(first, end):
        @pl.loop(first, end)
        def _(h):
            out_ref[0, :, columns(h)] = (attended[:, columns(h)] * squares[...]).astype(BF16)

    def along_seq(source, target, sends, receives, step, slot, arriving):
        peer = lax.rem(me + step, n)
        landing = peer if arriving else me
        return pltpu.make_async_remote_copy(
            src_ref=source.at[peer if slot else me],
            dst_ref=target.at[landing],
            send_sem=sends.at[step],
            recv_sem=receives.at[landing],
            device_id=(peer, rep),
            device_id_type=MESH,
        )

    def along_rep(step, arriving):
        peer = lax.rem(rep + step, reps)
        landing = peer if arriving else rep
        return pltpu.make_async_remote_copy(
            src_ref=norm_all.at[rep],
            dst_ref=norm_all.at[landing],
            send_sem=norm_send.at[step],
            recv_sem=norm_recv.at[landing],
            device_id=(me, peer),
            device_id_type=MESH,
        )

    @pl.when(me < last)
    def _():
        @pl.loop(0, per_owner)
        def _(c):
            to_owner(c, last).wait_recv()

    for i in range(share):
        cols = slice(i * HEAD_DIM, (i + 1) * HEAD_DIM)
        kept = dot(heard[:, cols], fin_ref[i], 1, 0, lax.Precision.HIGHEST)
        heard[:, cols] = gains[:, cols] * kept + fresh[:, cols]
    mine = heard[:steps, :]
    ssq_all[me] = jnp.broadcast_to(jnp.sum(mine * mine, axis=1, keepdims=True), (steps, HEAD_DIM))
    for step in range(1, n):
        along_seq(ssq_all, ssq_all, ssq_send, ssq_recv, step, False, False).start()
    cut = heads // 3
    scale_out(0, cut)
    for step in range(1, n):
        along_seq(ssq_all, ssq_all, ssq_send, ssq_recv, step, False, True).wait_recv()
    mean = jnp.sum(ssq_all[...], axis=0)[:, :1] / (heads * HEAD_DIM)
    norm_all[rep] = (mine * lax.rsqrt(mean + epsilon)).astype(BF16).astype(F32)
    for step in range(1, reps):
        along_rep(step, False).start()
    scale_out(cut, 2 * cut)
    for step in range(1, reps):
        along_rep(step, True).wait_recv()
    for r in range(reps):
        for s in range(steps):
            at = s * reps + r
            rows_in[at : at + 1, :] = norm_all[r, s : s + 1, :]
    projected = dot(rows_in[...].astype(BF16), w_ref[...], 1, 0)
    per = steps * reps // n
    for j in range(n):
        parts[j] = projected[j * per : (j + 1) * per, :]
    for step in range(1, n):
        along_seq(parts, parts_in, part_send, part_recv, step, True, False).start()
    parts_in[me] = parts[me]
    scale_out(2 * cut, heads)
    for step in range(1, n):
        along_seq(parts, parts_in, part_send, part_recv, step, True, True).wait_recv()
    sums[me] = jnp.sum(parts_in[...], axis=0)
    for step in range(1, n):
        along_seq(sums, sums, sum_send, sum_recv, step, False, False).start()
    for step in range(1, n):
        along_seq(sums, sums, sum_send, sum_recv, step, False, True).wait_recv()
    for j in range(n):
        rows_out[j * per : (j + 1) * per, :] = sums[j]
    step_ref[...] = rows_out[...].astype(BF16)

    for step in range(1, n):
        along_seq(ssq_all, ssq_all, ssq_send, ssq_recv, step, False, False).wait_send()
        along_seq(parts, parts_in, part_send, part_recv, step, True, False).wait_send()
        along_seq(sums, sums, sum_send, sum_recv, step, False, False).wait_send()
    for step in range(1, reps):
        along_rep(step, False).wait_send()

    @pl.when(me < last)
    def _():
        @pl.loop(0, chunks)
        def _(c):
            to_right(c).wait_send()

    @pl.when(me == last)
    def _():
        @pl.loop(0, chunks - per_owner)
        def _(c):
            to_owner(c, 0).wait_send()


def whole(lengths, query, key, value, decay, step_in, step_decay, weight):
    n, reps = lax.axis_size("seq"), lax.axis_size("rep")
    _, block, width = query.shape
    heads = width // HEAD_DIM
    share = heads // n
    chunk = min(CHUNK, share)
    steps, part_width = step_decay.shape[0], step_in.shape[1]
    out_columns = weight.shape[1]
    padded = 8 * pl.cdiv(steps, 8)
    hbm = pl.BlockSpec(memory_space=pltpu.HBM)
    rows = steps * reps
    vmem = pl.BlockSpec(memory_space=pltpu.VMEM)
    return pl.pallas_call(
        functools.partial(prompt_kernel, n, reps, heads, block),
        out_shape=(
            jax.ShapeDtypeStruct(query.shape, BF16),
            jax.ShapeDtypeStruct((rows, out_columns), BF16),
        ),
        in_specs=[pl.BlockSpec(memory_space=pltpu.SMEM)] + [hbm] * 4 + [vmem] * 2 + [hbm],
        out_specs=(vmem, vmem),
        scratch_shapes=[
            pltpu.VMEM(query.shape, BF16),
            pltpu.VMEM(key.shape, BF16),
            pltpu.VMEM(value.shape, BF16),
            pltpu.VMEM(decay.shape, F32),
            pltpu.VMEM(weight.shape, BF16),
            pltpu.SemaphoreType.DMA((5,)),
            pltpu.VMEM((padded, part_width), F32),
            pltpu.VMEM((padded, part_width), F32),
            pltpu.VMEM((share, HEAD_DIM, HEAD_DIM), F32),
            pltpu.VMEM((padded, part_width), F32),
            pltpu.VMEM((n, steps, HEAD_DIM), F32),
            pltpu.VMEM((reps, steps, part_width), F32),
            pltpu.VMEM((rows, part_width), F32),
            pltpu.VMEM((n, rows // n, out_columns), F32),
            pltpu.VMEM((n, rows // n, out_columns), F32),
            pltpu.VMEM((n, rows // n, out_columns), F32),
            pltpu.VMEM((rows, out_columns), F32),
            pltpu.VMEM((heads, block, HEAD_DIM), F32),
            pltpu.VMEM((heads, 1, block), F32),
            pltpu.VMEM((heads, 1, HEAD_DIM), F32),
            pltpu.VMEM((heads, HEAD_DIM, HEAD_DIM), F32),
            pltpu.VMEM((heads, HEAD_DIM, HEAD_DIM), F32),
            pltpu.VMEM((block, width), F32),
            pltpu.VMEM((block, HEAD_DIM), F32),
            pltpu.VMEM((block, HEAD_DIM), F32),
            pltpu.SemaphoreType.DMA((heads // chunk,)),
            pltpu.SemaphoreType.DMA((heads // chunk,)),
            pltpu.SemaphoreType.DMA((heads // chunk,)),
            pltpu.SemaphoreType.DMA((share // chunk,)),
            pltpu.SemaphoreType.DMA((n,)),
            pltpu.SemaphoreType.DMA((n,)),
            pltpu.SemaphoreType.DMA((reps,)),
            pltpu.SemaphoreType.DMA((reps,)),
            pltpu.SemaphoreType.DMA((n,)),
            pltpu.SemaphoreType.DMA((n,)),
            pltpu.SemaphoreType.DMA((n,)),
            pltpu.SemaphoreType.DMA((n,)),
        ],
        compiler_params=pltpu.CompilerParams(
            collective_id=0, has_side_effects=True, vmem_limit_bytes=63 * 1024 * 1024
        ),
    )(lengths, query, key, value, decay, step_in, step_decay, weight)


def shards(
    lengths,
    prompt_query,
    prompt_key,
    prompt_value,
    prompt_decay,
    step_query,
    step_key,
    step_value,
    step_decay,
    out_weight,
):
    wide = (-1, step_query.shape[2])
    step_in = jnp.concatenate(
        [part.reshape(wide).astype(F32) for part in (step_query, step_key, step_value)]
    )
    prompt_out, rows = whole(
        lengths,
        prompt_query,
        prompt_key,
        prompt_value,
        prompt_decay,
        step_in,
        step_decay,
        out_weight,
    )
    steps = step_query.shape[0]
    return (prompt_out, rows.reshape(steps, rows.shape[0] // steps, rows.shape[1]))


def solution(mesh):
    return jax.shard_map(
        shards,
        mesh=mesh,
        in_specs=(
            P("rep"),
            P("rep", "seq", None),
            P("rep", "seq", None),
            P("rep", "seq", None),
            P("rep", None, "seq"),
            P(None, "rep", "seq"),
            P(None, "rep", "seq"),
            P(None, "rep", "seq"),
            P(None, "rep", "seq"),
            P("seq", "rep"),
        ),
        out_specs=(P("rep", "seq", None), P(None, None, "rep")),
        check_vma=False,
    )
```

```python
import functools
import jax
import jax.numpy as jnp
from jax import lax
from jax.experimental import pallas as pl
from jax.experimental.pallas import tpu as pltpu
from jax.sharding import PartitionSpec as P

HEAD_DIM = 128
CHUNK = 1
epsilon = 1e-06
MESH = pl.DeviceIdType.MESH
F32 = jnp.float32
BF16 = jnp.bfloat16


def dot(a, b, ca, cb, precision=None):
    return lax.dot_general(
        a, b, (((ca,), (cb,)), ((), ())), preferred_element_type=F32, precision=precision
    )


def prompt_kernel(
    n, reps, heads, block,
    len_ref, q_hbm, k_hbm, v_hbm, d_hbm, sq_ref, sk_ref, sv_ref, sd_ref, w_hbm,
    out_ref, step_ref,
    q_ref, k_ref, v_ref, d_ref, w_ref, load_sem, gains, fresh, step_in,
    fin_ref, heard, ssq_all, norm_all, rows_in, parts, parts_in, sums, rows_out,
    cum_b, cum_row, total, state, inbox, attended, squares, live_b,
    send_sem, recv_sem, fin_send, fin_recv,
    ssq_send, ssq_recv, norm_send, norm_recv, part_send, part_recv, sum_send, sum_recv,
):
    me = lax.axis_index("seq")
    rep = lax.axis_index("rep")
    last = n - 1
    share = heads // n
    chunk = min(CHUNK, share)
    chunks = heads // chunk
    per_owner = share // chunk

    loads = [
        pltpu.make_async_copy(source, target, load_sem.at[i])
        for i, (source, target) in enumerate(
            (
                (d_hbm, d_ref),
                (k_hbm, k_ref),
                (v_hbm, v_ref),
                (q_hbm, q_ref),
                (w_hbm, w_ref),
            )
        )
    ]
    for load in loads:
        load.start()
    barrier = pltpu.get_barrier_semaphore()
    for step in range(1, n):
        pl.semaphore_signal(
            barrier, inc=1, device_id=(lax.rem(me + step, n), rep), device_id_type=MESH
        )

    for step in range(1, reps):
        pl.semaphore_signal(
            barrier, inc=1, device_id=(me, lax.rem(rep + step, reps)), device_id_type=MESH
        )

    length = len_ref[0]
    start = me * block
    row_live = (lax.broadcasted_iota(jnp.int32, (1, block), 1) + start < length).astype(F32)
    live_b[...] = (
        lax.broadcasted_iota(jnp.int32, (block, HEAD_DIM), 0) + start < length
    ).astype(F32)
    loads[0].wait()
    log_decay = d_ref[0] * row_live
    below = (
        lax.broadcasted_iota(jnp.int32, (block, block), 0)
        >= lax.broadcasted_iota(jnp.int32, (block, block), 1)
    ).astype(F32)
    cum = dot(log_decay, below, 1, 1, lax.Precision.HIGHEST)
    for h in range(heads):
        cum_row[h] = cum[h : h + 1, :]
    cum_t = dot(below, log_decay, 1, 1, lax.Precision.HIGHEST)
    for h in range(heads):
        cum_b[h] = jnp.broadcast_to(cum_t[:, h : h + 1], (block, HEAD_DIM))
        total[h] = cum_b[h, block - 1 :, :]

    def columns(h):
        return pl.ds(pl.multiple_of(h * HEAD_DIM, HEAD_DIM), HEAD_DIM)

    def to_right(c):
        part = pl.ds(c * chunk, chunk)
        return pltpu.make_async_remote_copy(
            src_ref=state.at[part],
            dst_ref=inbox.at[part],
            send_sem=send_sem.at[c],
            recv_sem=recv_sem.at[c],
            device_id=(lax.rem(me + 1, n), rep),
            device_id_type=MESH,
        )

    def to_owner(c, owner):
        return pltpu.make_async_remote_copy(
            src_ref=state.at[pl.ds(c * chunk, chunk)],
            dst_ref=fin_ref.at[pl.ds((c % per_owner) * chunk, chunk)],
            send_sem=fin_send.at[c],
            recv_sem=fin_recv.at[c % per_owner],
            device_id=(owner, rep),
            device_id_type=MESH,
        )

    loads[1].wait()
    loads[2].wait()
    pl.semaphore_wait(barrier, n - 1 + reps - 1)

    @pl.loop(0, chunks)
    def _(c):
        for i in range(chunk):
            h = c * chunk + i
            keys = k_ref[0, :, columns(h)].astype(F32) * live_b[...]
            scaled = (keys * jnp.exp(total[h] - cum_b[h])).astype(BF16)
            state[h] = dot(scaled, v_ref[0, :, columns(h)], 0, 0)

        @pl.when(me == 0)
        def _():
            to_right(c).start()

    loads[3].wait()
    loads[4].wait()
    steps = sq_ref.shape[0]
    for i, part in enumerate((sq_ref, sk_ref, sv_ref)):
        step_in[i * steps : (i + 1) * steps, :] = part[...].astype(F32)
    heard[...] = jnp.zeros_like(heard)
    gains[...] = jnp.zeros_like(gains)
    fresh[...] = jnp.zeros_like(fresh)
    heard[:steps, :] = step_in[:steps, :]
    for i in range(share):
        cols = slice(i * HEAD_DIM, (i + 1) * HEAD_DIM)
        cums = []
        for s in range(steps):
            one = sd_ref[s, :, i : i + 1]
            cums.append(one if s == 0 else cums[-1] + one)
            row = jnp.zeros((1, HEAD_DIM), F32)
            for j in range(s + 1):
                met = step_in[s : s + 1, cols] * step_in[steps + j : steps + j + 1, cols]
                meet = jnp.sum(met, axis=1, keepdims=True) * jnp.exp(cums[s] - cums[j])
                row = row + meet * step_in[2 * steps + j : 2 * steps + j + 1, cols]
            fresh[s : s + 1, cols] = row
            gains[s : s + 1, cols] = jnp.broadcast_to(jnp.exp(cums[s]), (1, HEAD_DIM))

    tile = HEAD_DIM
    tiles = block // tile
    causal = (
        lax.broadcasted_iota(jnp.int32, (tile, tile), 0)
        >= lax.broadcasted_iota(jnp.int32, (tile, tile), 1)
    )
    squares[...] = jnp.zeros_like(squares)

    @pl.when(me == 0)
    def _():
        inbox[...] = jnp.zeros_like(inbox)

    def forward(c):
        @pl.when(me > 0)
        def _():
            to_right(c).wait_recv()
            for i in range(chunk):
                h = c * chunk + i
                state[h] = inbox[h] * jnp.exp(total[h]) + state[h]

            @pl.when(me < last)
            def _():
                to_right(c).start()

            @pl.when(me == last)
            def _():
                owner = c // per_owner

                @pl.when(owner != last)
                def _():
                    to_owner(c, owner).start()

                @pl.when(owner == last)
                def _():
                    fin_ref[pl.ds((c % per_owner) * chunk, chunk)] = state[
                        pl.ds(c * chunk, chunk)
                    ]

    def attend(c):
        for i in range(chunk):
            h = c * chunk + i
            query = q_ref[0, :, columns(h)]
            keys = (k_ref[0, :, columns(h)].astype(F32) * live_b[...]).astype(BF16)
            values = v_ref[0, :, columns(h)]
            carried = jnp.exp(cum_b[h]) * dot(query, inbox[h].astype(BF16), 1, 0)
            for t in range(tiles):
                rows = slice(t * tile, (t + 1) * tile)
                width = (t + 1) * tile
                scores = dot(query[rows], keys[:width], 1, 1)
                pieces = []
                for s in range(t + 1):
                    cols = slice(s * tile, (s + 1) * tile)
                    gap = cum_b[h, rows, :] - cum_row[h, :, cols]
                    if s == t:
                        decay = jnp.where(causal, jnp.exp(jnp.where(causal, gap, 0.0)), 0.0)
                    else:
                        decay = jnp.exp(gap)
                    pieces.append((scores[:, cols] * decay).astype(BF16))
                mixed = pieces[0] if t == 0 else jnp.concatenate(pieces, axis=1)
                both = dot(mixed, values[:width], 1, 0) + carried[rows]
                attended[rows, columns(h)] = both
                squares[rows, :] += both * both

    half = chunks // 2
    quarter = half // 4

    @pl.loop(0, half)
    def _(c):
        forward(c)
        attend(c)

    @pl.loop(half, chunks)
    def _(c):
        forward(c)

    def attend_part(part):
        pl.loop(half + part * quarter, chunks if part == 3 else half + (part + 1) * quarter)(attend)

    def along_seq(source, target, sends, receives, step, slot, arriving):
        peer = lax.rem(me + step, n)
        landing = peer if arriving else me
        return pltpu.make_async_remote_copy(
            src_ref=source.at[peer if slot else me],
            dst_ref=target.at[landing],
            send_sem=sends.at[step],
            recv_sem=receives.at[landing],
            device_id=(peer, rep),
            device_id_type=MESH,
        )

    def along_rep(step, arriving):
        peer = lax.rem(rep + step, reps)
        landing = peer if arriving else rep
        return pltpu.make_async_remote_copy(
            src_ref=norm_all.at[rep],
            dst_ref=norm_all.at[landing],
            send_sem=norm_send.at[step],
            recv_sem=norm_recv.at[landing],
            device_id=(me, peer),
            device_id_type=MESH,
        )

    @pl.when(me < last)
    def _():
        @pl.loop(0, per_owner)
        def _(c):
            to_owner(c, last).wait_recv()

    for i in range(share):
        cols = slice(i * HEAD_DIM, (i + 1) * HEAD_DIM)
        kept = dot(heard[:, cols], fin_ref[i], 1, 0, lax.Precision.HIGHEST)
        heard[:, cols] = gains[:, cols] * kept + fresh[:, cols]
    mine = heard[:steps, :]
    ssq_all[me] = jnp.broadcast_to(jnp.sum(mine * mine, axis=1, keepdims=True), (steps, HEAD_DIM))
    for step in range(1, n):
        along_seq(ssq_all, ssq_all, ssq_send, ssq_recv, step, False, False).start()
    attend_part(0)
    for step in range(1, n):
        along_seq(ssq_all, ssq_all, ssq_send, ssq_recv, step, False, True).wait_recv()
    mean = jnp.sum(ssq_all[...], axis=0)[:, :1] / (heads * HEAD_DIM)
    norm_all[rep] = (mine * lax.rsqrt(mean + epsilon)).astype(BF16).astype(F32)
    for step in range(1, reps):
        along_rep(step, False).start()
    attend_part(1)
    for step in range(1, reps):
        along_rep(step, True).wait_recv()
    for r in range(reps):
        for s in range(steps):
            at = s * reps + r
            rows_in[at : at + 1, :] = norm_all[r, s : s + 1, :]
    projected = dot(rows_in[...].astype(BF16), w_ref[...], 1, 0)
    per = steps * reps // n
    for j in range(n):
        parts[j] = projected[j * per : (j + 1) * per, :]
    for step in range(1, n):
        along_seq(parts, parts_in, part_send, part_recv, step, True, False).start()
    parts_in[me] = parts[me]
    attend_part(2)
    for step in range(1, n):
        along_seq(parts, parts_in, part_send, part_recv, step, True, True).wait_recv()
    sums[me] = jnp.sum(parts_in[...], axis=0)
    for step in range(1, n):
        along_seq(sums, sums, sum_send, sum_recv, step, False, False).start()
    attend_part(3)
    for t in range(tiles):
        rows = slice(t * tile, (t + 1) * tile)
        mean = jnp.sum(squares[rows, :], axis=1, keepdims=True) / (heads * HEAD_DIM)
        scale = jnp.broadcast_to(lax.rsqrt(mean + epsilon), (tile, HEAD_DIM)) * live_b[rows, :]
        squares[rows, :] = scale

    @pl.loop(0, heads)
    def _(h):
        out_ref[0, :, columns(h)] = (attended[:, columns(h)] * squares[...]).astype(BF16)

    for step in range(1, n):
        along_seq(sums, sums, sum_send, sum_recv, step, False, True).wait_recv()
    for j in range(n):
        rows_out[j * per : (j + 1) * per, :] = sums[j]
    for s in range(steps):
        step_ref[s] = rows_out[s * reps : (s + 1) * reps, :].astype(BF16)

    for step in range(1, n):
        along_seq(ssq_all, ssq_all, ssq_send, ssq_recv, step, False, False).wait_send()
        along_seq(parts, parts_in, part_send, part_recv, step, True, False).wait_send()
        along_seq(sums, sums, sum_send, sum_recv, step, False, False).wait_send()
    for step in range(1, reps):
        along_rep(step, False).wait_send()

    @pl.when(me < last)
    def _():
        @pl.loop(0, chunks)
        def _(c):
            to_right(c).wait_send()

    @pl.when(me == last)
    def _():
        @pl.loop(0, chunks - per_owner)
        def _(c):
            to_owner(c, 0).wait_send()


def whole(lengths, query, key, value, decay, step_q, step_k, step_v, step_decay, weight):
    n, reps = lax.axis_size("seq"), lax.axis_size("rep")
    _, block, width = query.shape
    heads = width // HEAD_DIM
    share = heads // n
    chunk = min(CHUNK, share)
    steps, part_width = step_decay.shape[0], step_q.shape[1]
    out_columns = weight.shape[1]
    padded = 8 * pl.cdiv(steps, 8)
    hbm = pl.BlockSpec(memory_space=pltpu.HBM)
    rows = steps * reps
    vmem = pl.BlockSpec(memory_space=pltpu.VMEM)
    return pl.pallas_call(
        functools.partial(prompt_kernel, n, reps, heads, block),
        out_shape=(
            jax.ShapeDtypeStruct(query.shape, BF16),
            jax.ShapeDtypeStruct((steps, reps, out_columns), BF16),
        ),
        in_specs=[pl.BlockSpec(memory_space=pltpu.SMEM)] + [hbm] * 4 + [vmem] * 4 + [hbm],
        out_specs=(vmem, vmem),
        scratch_shapes=[
            pltpu.VMEM(query.shape, BF16),
            pltpu.VMEM(key.shape, BF16),
            pltpu.VMEM(value.shape, BF16),
            pltpu.VMEM(decay.shape, F32),
            pltpu.VMEM(weight.shape, BF16),
            pltpu.SemaphoreType.DMA((5,)),
            pltpu.VMEM((padded, part_width), F32),
            pltpu.VMEM((padded, part_width), F32),
            pltpu.VMEM((3 * steps, part_width), F32),
            pltpu.VMEM((share, HEAD_DIM, HEAD_DIM), F32),
            pltpu.VMEM((padded, part_width), F32),
            pltpu.VMEM((n, steps, HEAD_DIM), F32),
            pltpu.VMEM((reps, steps, part_width), F32),
            pltpu.VMEM((rows, part_width), F32),
            pltpu.VMEM((n, rows // n, out_columns), F32),
            pltpu.VMEM((n, rows // n, out_columns), F32),
            pltpu.VMEM((n, rows // n, out_columns), F32),
            pltpu.VMEM((rows, out_columns), F32),
            pltpu.VMEM((heads, block, HEAD_DIM), F32),
            pltpu.VMEM((heads, 1, block), F32),
            pltpu.VMEM((heads, 1, HEAD_DIM), F32),
            pltpu.VMEM((heads, HEAD_DIM, HEAD_DIM), F32),
            pltpu.VMEM((heads, HEAD_DIM, HEAD_DIM), F32),
            pltpu.VMEM((block, width), F32),
            pltpu.VMEM((block, HEAD_DIM), F32),
            pltpu.VMEM((block, HEAD_DIM), F32),
            pltpu.SemaphoreType.DMA((heads // chunk,)),
            pltpu.SemaphoreType.DMA((heads // chunk,)),
            pltpu.SemaphoreType.DMA((heads // chunk,)),
            pltpu.SemaphoreType.DMA((share // chunk,)),
            pltpu.SemaphoreType.DMA((n,)),
            pltpu.SemaphoreType.DMA((n,)),
            pltpu.SemaphoreType.DMA((reps,)),
            pltpu.SemaphoreType.DMA((reps,)),
            pltpu.SemaphoreType.DMA((n,)),
            pltpu.SemaphoreType.DMA((n,)),
            pltpu.SemaphoreType.DMA((n,)),
            pltpu.SemaphoreType.DMA((n,)),
        ],
        compiler_params=pltpu.CompilerParams(
            collective_id=0, has_side_effects=True, vmem_limit_bytes=63 * 1024 * 1024
        ),
    )(lengths, query, key, value, decay, step_q, step_k, step_v, step_decay, weight)


def shards(
    lengths,
    prompt_query,
    prompt_key,
    prompt_value,
    prompt_decay,
    step_query,
    step_key,
    step_value,
    step_decay,
    out_weight,
):
    wide = (-1, step_query.shape[2])
    prompt_out, step_out = whole(
        lengths,
        prompt_query,
        prompt_key,
        prompt_value,
        prompt_decay,
        step_query.reshape(wide),
        step_key.reshape(wide),
        step_value.reshape(wide),
        step_decay,
        out_weight,
    )
    return (prompt_out, step_out)


def solution(mesh):
    return jax.shard_map(
        shards,
        mesh=mesh,
        in_specs=(
            P("rep"),
            P("rep", "seq", None),
            P("rep", "seq", None),
            P("rep", "seq", None),
            P("rep", None, "seq"),
            P(None, "rep", "seq"),
            P(None, "rep", "seq"),
            P(None, "rep", "seq"),
            P(None, "rep", "seq"),
            P("seq", "rep"),
        ),
        out_specs=(P("rep", "seq", None), P(None, None, "rep")),
        check_vma=False,
    )
```
